256 devices in a mesh: section: 32 (over y, x, z_lo), tensor: 8 (over z_hi, core).
Axes of the slice: x: 4, y: 4, z: 8 (z_hi: 4, z_lo: 2; z = z_hi * 2 + z_lo), core: 2. Of those that a mesh axis runs over, the one named last changes fastest.
Arguments:
- layer_inputs: bfloat16 [32, 256, 1536], P('section', 'tensor'), may hold values from -6 to 6
- output_grads: bfloat16 [32, 256, 1536], P('section', 'tensor'), may hold values from -6 to 6
- held_inputs: bfloat16 [32, 2, 256, 1536], P('section', None, 'tensor'), may hold values from -6 to 6
- held_qkv: bfloat16 [32, 3, 256, 1536], P('section', None, None, 'tensor'), may hold values from -120 to 120
- held_gateup: bfloat16 [32, 2, 256, 3072], P('section', None, None, 'tensor'), may hold values from -6 to 6
- swapped_pairs: int32 [16], replicated, may hold values 0 or 1
- w_qkv: bfloat16 [32, 3, 1536, 1536], P('section', None, None, 'tensor'), may hold values from -14 to 14
- w_out: bfloat16 [32, 1536, 1536], P('section', 'tensor'), may hold values from -0.15625 to 0.15625
- w_gateup: bfloat16 [32, 2, 1536, 3072], P('section', None, None, 'tensor'), may hold values from -0.15625 to 0.15625
- w_down: bfloat16 [32, 3072, 1536], P('section', 'tensor'), may hold values from -0.109375 to 0.109375
- norm_gains: float32 [32, 2, 1536], P('section'), may hold values from 0.5 to 1.5
Outputs:
- forward_sent: bfloat16 [32, 256, 1536], P('section', 'tensor')
- backward_sent: bfloat16 [32, 256, 1536], P('section', 'tensor')
- stash_inputs: bfloat16 [32, 2, 256, 1536], P('section', None, 'tensor')
- stash_qkv: bfloat16 [32, 3, 256, 1536], P('section', None, None, 'tensor')
- stash_gateup: bfloat16 [32, 2, 256, 3072], P('section', None, None, 'tensor')
- grad_qkv: bfloat16 [32, 3, 1536, 1536], P('section', None, None, 'tensor')
- grad_out: bfloat16 [32, 1536, 1536], P('section', 'tensor')
- grad_gateup: bfloat16 [32, 2, 1536, 3072], P('section', None, None, 'tensor')
- grad_down: bfloat16 [32, 3072, 1536], P('section', 'tensor')
- grad_gains: float32 [32, 2, 1536], P('section')
The draws below stay inside these ranges and needn't reach their ends.
Inputs may be any that keep to these rules, and one draw needn't show every extreme that they name: `swapped_pairs`: 1 marks a pair of sections i and 31 - i whose stashes each sit on the other device of the pair.
All inputs are finite; a program needn't handle non-finite values.
Results may differ from the reference program's by a relative error of at most 0.023.
Values may be sent and summed in bfloat16 or wider, within the bound.
No kernel may reach another device: no remote copies, remote signals or barrier semaphores. Data moves between devices by JAX's collectives and lax.ppermute only.
A program may use at most 128 MiB of HBM per device.

```python
import jax
import jax.numpy as jnp
from jax import lax

D = 1536
HEADS = 16
FF = 3072
SEQ = 256
N_SECTION = 32


def draw_held_qkv(key, part):
    key = jax.random.fold_in(key, 11)
    base = jax.random.truncated_normal(jax.random.fold_in(key, 1), -4.5, 4.5, (N_SECTION, 3, SEQ, D), jnp.float32)
    return base.astype(jnp.bfloat16)


def draw_w_qkv(key, part):
    key = jax.random.fold_in(key, 7)
    base = jax.random.truncated_normal(jax.random.fold_in(key, 1), -4.5, 4.5, (N_SECTION, 3, D, D), jnp.float32) * D ** (-0.5)
    return base.astype(jnp.bfloat16)


def plant(array, stream_key, smallest, high):
    extent = array.shape
    spot = [jax.random.randint(jax.random.fold_in(stream_key, axis), (), 0, extent[axis]) for axis in range(len(extent))]
    array = array.at[tuple(spot)].set(smallest)
    longest = extent.index(max(extent))
    spot[longest] = (spot[longest] + 1) % extent[longest]
    return array.at[tuple(spot)].set(high)


def block_scale(key, dims, split, low, high):
    gain = 1.0
    for dim, shards_of in split:
        steps = jax.random.uniform(jax.random.fold_in(jax.random.fold_in(key, 6), dim), (shards_of,), jnp.float32, low / len(split), high / len(split))
        gain = gain * jnp.repeat(jnp.exp(steps), dims[dim] // shards_of).reshape((-1,) + (1,) * (len(dims) - 1 - dim))
    return gain


def normal_values(own_key, shape, scale, bound, pieces=(), held_as=jnp.bfloat16):
    entries = scale * jax.random.normal(own_key, shape, jnp.float32)
    if pieces:
        entries = entries * block_scale(own_key, shape, pieces, -0.22, 0.18)
    return jnp.clip(entries, -bound, bound).astype(held_as)


def setup_inputs(seed: int = 0) -> dict:
    key_of = jax.random.split(jax.random.key(seed), 12)
    layer_inputs = normal_values(key_of[0], (N_SECTION, SEQ, D), 1.0, 6.0, ((0, 32), (1, 8)))
    output_grads = normal_values(key_of[1], (N_SECTION, SEQ, D), 1.0, 6.0, ((0, 32), (1, 8)))
    held_inputs = normal_values(key_of[2], (N_SECTION, 2, SEQ, D), 1.0, 6.0, ((0, 32), (2, 8)))
    held_qkv = draw_held_qkv(jax.random.fold_in(key_of[11], 71), 0)
    held_gateup = normal_values(key_of[4], (N_SECTION, 2, SEQ, FF), 1.0, 6.0, ((0, 32), (3, 8)))
    swapped_pairs = plant((jax.random.randint(key_of[5], (N_SECTION // 2,), 0, 2) < 1).astype(jnp.int32), jax.random.fold_in(key_of[5], 1), 0, 1)
    w_qkv = draw_w_qkv(jax.random.fold_in(key_of[11], 71), 0)
    w_out = normal_values(key_of[7], (N_SECTION, D, D), D ** -0.5, 0.15625, ((0, 32), (1, 8)))
    w_gateup = normal_values(key_of[8], (N_SECTION, 2, D, FF), D ** -0.5, 0.15625, ((0, 32), (3, 8)))
    w_down = normal_values(key_of[9], (N_SECTION, FF, D), FF ** -0.5, 0.109375, ((0, 32), (1, 8)))
    norm_gains = jnp.clip(1.0 + 0.1 * jax.random.normal(key_of[10], (N_SECTION, 2, D), jnp.float32), 0.5, 1.5)
    return dict(layer_inputs=layer_inputs, output_grads=output_grads, held_inputs=held_inputs, held_qkv=held_qkv, held_gateup=held_gateup, swapped_pairs=swapped_pairs, w_qkv=w_qkv, w_out=w_out, w_gateup=w_gateup, w_down=w_down, norm_gains=norm_gains)


EPSILON = 1e-05

def rms_scale(matrix, gain_row):
    values_f = matrix.astype(jnp.float32)
    inverse = lax.rsqrt(lax.optimization_barrier(jnp.mean(values_f * values_f, axis=-1, keepdims=True)) + EPSILON)
    return values_f * inverse * gain_row

def norm_back(matrix, gain_row, upstream):
    values_f = matrix.astype(jnp.float32)
    inverse = lax.rsqrt(lax.optimization_barrier(jnp.mean(values_f * values_f, axis=-1, keepdims=True)) + EPSILON)
    normal = values_f * inverse
    scaled_grad = upstream * gain_row
    inner = lax.optimization_barrier(jnp.mean(scaled_grad * normal, axis=-1, keepdims=True))
    return (inverse * (scaled_grad - normal * inner), upstream * normal)

def attend(qkv_rows):
    head_size = D // HEADS
    length = qkv_rows.shape[1]
    head_count = qkv_rows.shape[2] // head_size
    split_rows = qkv_rows.astype(jnp.float32).reshape(3, length, head_count, head_size)
    scores = jnp.einsum('thd,shd->hts', split_rows[0], split_rows[1]) * head_size ** (-0.5)
    causal_mask = jnp.arange(length)[:, None] >= jnp.arange(length)[None, :]
    scores = jnp.where(causal_mask[None], scores, -1e+30)
    probs_full = jax.nn.softmax(scores, axis=-1)
    probs_low = probs_full.astype(jnp.bfloat16)
    mixed = jnp.einsum('hts,shd->thd', probs_low.astype(jnp.float32), split_rows[2])
    return (probs_full, probs_low, mixed.reshape(length, head_count * head_size).astype(jnp.bfloat16))

def forward_layer(layer_in, wqkv, wout, wgateup, wdown, gain_pair):
    norm_in = rms_scale(layer_in, gain_pair[0]).astype(jnp.bfloat16)
    fwd_qkv = jnp.einsum('td,cde->cte', norm_in.astype(jnp.float32), wqkv.astype(jnp.float32)).astype(jnp.bfloat16)
    unused_a, unused_b, mixed = attend(fwd_qkv)
    mid_rows = (layer_in.astype(jnp.float32) + jnp.dot(mixed, wout, preferred_element_type=jnp.float32)).astype(jnp.bfloat16)
    norm_mid = rms_scale(mid_rows, gain_pair[1]).astype(jnp.bfloat16)
    fwd_gateup = jnp.einsum('td,cdf->ctf', norm_mid.astype(jnp.float32), wgateup.astype(jnp.float32)).astype(jnp.bfloat16)
    gate_f = fwd_gateup[0].astype(jnp.float32)
    act_low = (jax.nn.silu(gate_f) * fwd_gateup[1].astype(jnp.float32)).astype(jnp.bfloat16)
    layer_out = (mid_rows.astype(jnp.float32) + jnp.dot(act_low, wdown, preferred_element_type=jnp.float32)).astype(jnp.bfloat16)
    return (layer_out, mid_rows, fwd_qkv, fwd_gateup)

def backward_layer(grad_rows, input_rows, mid_rows, qkv_rows, gateup_rows, wqkv, wout, wgateup, wdown, gain_pair):
    head_size = D // HEADS
    length = grad_rows.shape[0]
    gate_f = gateup_rows[0].astype(jnp.float32)
    up_f = gateup_rows[1].astype(jnp.float32)
    sigmoid_gate = jax.nn.sigmoid(gate_f)
    silu_gate = gate_f * sigmoid_gate
    act_low = (silu_gate * up_f).astype(jnp.bfloat16)
    grad_down = jnp.dot(act_low.T, grad_rows, preferred_element_type=jnp.float32).astype(jnp.bfloat16)
    dact = jnp.dot(grad_rows, wdown.T, preferred_element_type=jnp.float32)
    dgate = dact * up_f * sigmoid_gate * (1.0 + gate_f * (1.0 - sigmoid_gate))
    dgateup = jnp.stack([dgate, dact * silu_gate]).astype(jnp.bfloat16)
    norm_mid = rms_scale(mid_rows, gain_pair[1]).astype(jnp.bfloat16)
    grad_gateup = jnp.einsum('td,ctf->cdf', norm_mid.astype(jnp.float32), dgateup.astype(jnp.float32)).astype(jnp.bfloat16)
    dnorm_mid = jnp.einsum('ctf,cdf->td', dgateup.astype(jnp.float32), wgateup.astype(jnp.float32))
    dmid_part, gain_mid_terms = norm_back(mid_rows, gain_pair[1], dnorm_mid)
    dmid = (grad_rows.astype(jnp.float32) + dmid_part).astype(jnp.bfloat16)
    dmixed = jnp.dot(dmid, wout.T, preferred_element_type=jnp.float32).astype(jnp.bfloat16)
    probs_full, probs_low, mixed = attend(qkv_rows)
    grad_out = jnp.dot(mixed.T, dmid, preferred_element_type=jnp.float32).astype(jnp.bfloat16)
    split_rows = qkv_rows.astype(jnp.float32).reshape(3, length, HEADS, head_size)
    dmixed_heads = dmixed.astype(jnp.float32).reshape(length, HEADS, head_size)
    dvalues = jnp.einsum('hts,thd->shd', probs_low.astype(jnp.float32), dmixed_heads)
    dprob = jnp.einsum('thd,shd->hts', dmixed_heads, split_rows[2])
    dscore = (probs_full * (dprob - lax.optimization_barrier(jnp.sum(dprob * probs_full, axis=-1, keepdims=True))) * head_size ** (-0.5)).astype(jnp.bfloat16).astype(jnp.float32)
    dqueries = jnp.einsum('hts,shd->thd', dscore, split_rows[1])
    dkeys = jnp.einsum('hts,thd->shd', dscore, split_rows[0])
    dqkv = jnp.stack([dqueries, dkeys, dvalues]).reshape(3, length, D).astype(jnp.bfloat16)
    norm_in = rms_scale(input_rows, gain_pair[0]).astype(jnp.bfloat16)
    grad_qkv = jnp.einsum('td,cte->cde', norm_in.astype(jnp.float32), dqkv.astype(jnp.float32)).astype(jnp.bfloat16)
    dnorm_in = jnp.einsum('cte,cde->td', dqkv.astype(jnp.float32), wqkv.astype(jnp.float32))
    din_part, gain_in_terms = norm_back(input_rows, gain_pair[0], dnorm_in)
    dinput = (dmid.astype(jnp.float32) + din_part).astype(jnp.bfloat16)
    grad_gains = jnp.stack([lax.optimization_barrier(jnp.sum(gain_in_terms, axis=0)), lax.optimization_barrier(jnp.sum(gain_mid_terms, axis=0))])
    return (dinput, grad_qkv, grad_out, grad_gateup, grad_down, grad_gains)

def reference(layer_inputs, output_grads, held_inputs, held_qkv, held_gateup, swapped_pairs, w_qkv, w_out, w_gateup, w_down, norm_gains):
    pair_flag = jnp.concatenate([swapped_pairs, swapped_pairs[::-1]]) > 0

    def place(stacked):
        flags = pair_flag.reshape((N_SECTION,) + (1,) * (stacked.ndim - 1))
        return jnp.where(flags, stacked[::-1], stacked)
    stash_x = place(held_inputs)
    stash_q = place(held_qkv)
    stash_g = place(held_gateup)

    def one_section(packed):
        layer_in, grad_rows, stash_pair, qkv_rows, gateup_rows, wqkv, wout, wgateup, wdown, gain_pair = packed
        layer_out, mid_rows, fwd_qkv, fwd_gateup = forward_layer(layer_in, wqkv, wout, wgateup, wdown, gain_pair)
        backs = backward_layer(grad_rows, stash_pair[0], stash_pair[1], qkv_rows, gateup_rows, wqkv, wout, wgateup, wdown, gain_pair)
        return (layer_out, mid_rows, fwd_qkv, fwd_gateup) + backs
    results = lax.map(one_section, (layer_inputs, output_grads, stash_x, stash_q, stash_g, w_qkv, w_out, w_gateup, w_down, norm_gains))
    layer_out, mid_rows, fwd_qkv, fwd_gateup, dinput, grad_qkv, grad_out, grad_gateup, grad_down, grad_gains = results
    zero_block = jnp.zeros((1, SEQ, D), jnp.bfloat16)
    forward_sent = jnp.concatenate([zero_block, layer_out[:-1]], axis=0)
    backward_sent = jnp.concatenate([dinput[1:], zero_block], axis=0)
    stash_inputs = place(jnp.stack([layer_inputs, mid_rows], axis=1))
    stash_qkv = place(fwd_qkv)
    stash_gateup = place(fwd_gateup)
    return (forward_sent, backward_sent, stash_inputs, stash_qkv, stash_gateup, grad_qkv, grad_out, grad_gateup, grad_down, grad_gains)
```

```python
import functools

import jax
import jax.numpy as jnp
from jax import lax
from jax.experimental import pallas as pl
from jax.experimental.pallas import tpu as pltpu
from jax.sharding import PartitionSpec as P

D = 1536
HEADS = 16
HEAD = D // HEADS
EPSILON = 1e-05
BF = jnp.bfloat16
F32 = jnp.float32
NN = ((1,), (0,))
NT = ((1,), (1,))
TN = ((0,), (0,))


def dot(a, b, dims):
    return lax.dot_general(a, b, (dims, ((), ())), preferred_element_type=F32)


def tensor_pairs(step_even, step_odd):
    return [
        (t, ((t // 2 + (step_odd if t % 2 else step_even)) % 4) * 2 + t % 2) for t in range(8)
    ]


CORE = [(t, t ^ 1) for t in range(8)]
GATHER = tensor_pairs(1, -1)
REDUCE = tensor_pairs(-1, 1)


def over(value, pairs):
    return lax.ppermute(value, "tensor", pairs)


def gather(block):
    both = jnp.stack([block, over(block, CORE)])
    near = over(both, GATHER)
    far = over(near[0], GATHER)
    return both, near, far, over(near, CORE), over(far, CORE)


def reduce_blocks(own, keep, send):
    got = over(send, CORE)
    held = keep.astype(F32) + got.astype(F32)
    far = over(held[2].astype(BF), REDUCE)
    near = over(jnp.stack([held[0] + far.astype(F32), held[1]]).astype(BF), REDUCE)
    sums = own.astype(F32) + near.astype(F32)
    return sums[0], over(sums[1].astype(BF), CORE)


def all_sum(value):
    for pairs in (CORE, [(t, t ^ 2) for t in range(8)], [(t, t ^ 4) for t in range(8)]):
        value = value + over(value, pairs)
    return value


def call(body, name, outs, scratch, flops, args):
    smem, vmem = pl.BlockSpec(memory_space=pltpu.SMEM), pl.BlockSpec(memory_space=pltpu.VMEM)
    moved = sum(a.size * a.dtype.itemsize for a in args)
    moved += sum(o.size * o.dtype.itemsize for o in outs)
    return pl.pallas_call(
        body,
        name=name,
        out_shape=outs,
        in_specs=[smem if a.dtype == jnp.int32 else vmem for a in args],
        out_specs=[vmem] * len(outs),
        scratch_shapes=scratch,
        cost_estimate=pl.CostEstimate(flops=flops, bytes_accessed=moved, transcendentals=0),
        compiler_params=pltpu.CompilerParams(vmem_limit_bytes=40 * 2**20),
    )(*args)


def shape(*dims, dtype=BF):
    return jax.ShapeDtypeStruct(dims, dtype)


def row_norm(block, gain):
    values = block.astype(F32)
    inverse = lax.rsqrt(jnp.mean(values * values, axis=-1, keepdims=True) + EPSILON)
    return values * inverse * gain


def fill(full, off, both, near, far, near_s, far_s, pick, change):
    blocks = [
        functools.partial(pick, both, 0),
        functools.partial(pick, both, 1),
        functools.partial(pick, near, 0),
        functools.partial(pick, near, 1),
        functools.partial(pick, far, None),
        functools.partial(pick, near_s, 0),
        functools.partial(pick, near_s, 1),
        functools.partial(pick, far_s, None),
    ]
    for i, block in enumerate(blocks):
        full[pl.ds(pl.multiple_of(off[i], 32), 32), :] = change(block())


def pick_at(index):
    def pick(ref, lead):
        where = () if lead is None else (lead,)
        where = where if index is None else where + (index,)
        return ref[where] if where else ref[...]

    return pick


def spread(total, off, own, keep, send):
    for i in range(8):
        rows = total[pl.ds(pl.multiple_of(off[i], 32), 32), :].astype(BF)
        if i < 2:
            own[i] = rows
        elif i < 5:
            keep[i - 2] = rows
        else:
            send[i - 5] = rows


SPREAD = [shape(2, 32, D), shape(3, 32, D), shape(3, 32, D)]


def probs_of(keys, queries):
    scores = dot(keys, queries, TN) * HEAD ** (-0.5)
    length = scores.shape[0]
    key = lax.broadcasted_iota(jnp.int32, (length, length), 0)
    query = lax.broadcasted_iota(jnp.int32, (length, length), 1)
    scores = jnp.where(key <= query, scores, -1e30)
    powers = jnp.exp(scores - jnp.max(scores, axis=0, keepdims=True))
    return powers / jnp.sum(powers, axis=0, keepdims=True)


def forward_attention(
    off, both, near, far, near_s, far_s, gains, wqkv, wout, qkv, own, keep, send, full, mixed, total
):
    gain = gains[0:1, :]
    fill(full, off, both, near, far, near_s, far_s, pick_at(None), lambda b: row_norm(b, gain).astype(BF))
    for c in range(3):
        qkv[c] = dot(wqkv[c], full[...], NT).astype(BF)
    for h in range(2):
        rows = pl.ds(h * HEAD, HEAD)
        probs = probs_of(qkv[1, rows, :], qkv[0, rows, :]).astype(BF)
        mixed[rows, :] = dot(qkv[2, rows, :], probs, NN).astype(BF)
    total[...] = dot(mixed[...], wout[...], TN)
    spread(total, off, own, keep, send)


def forward_mlp(
    off, both, near, far, near_s, far_s, gains, wgateup, wdown, gateup, own, keep, send, full, total
):
    gain = gains[1:2, :]
    fill(full, off, both, near, far, near_s, far_s, pick_at(None), lambda b: row_norm(b, gain).astype(BF))
    for c in range(2):
        gateup[c] = dot(full[...], wgateup[c], NN).astype(BF)
    gate = gateup[0].astype(F32)
    act = (gate * jax.nn.sigmoid(gate) * gateup[1].astype(F32)).astype(BF)
    total[...] = dot(act, wdown[...], NN)
    spread(total, off, own, keep, send)


def backward_mlp(
    off, flag, both, near, far, near_s, far_s, held, fetched, wgateup, wdown,
    dgateup, act_low, grads, own, keep, send, total,
):
    fill(grads, off, both, near, far, near_s, far_s, pick_at(None), lambda b: b)
    moved = flag[0] > 0
    gate = jnp.where(moved, fetched[0], held[0]).astype(F32)
    up = jnp.where(moved, fetched[1], held[1]).astype(F32)
    sig = jax.nn.sigmoid(gate)
    silu = gate * sig
    act_low[...] = (silu * up).astype(BF)
    dact = dot(grads[...], wdown[...], NT)
    dgateup[0] = (dact * up * sig * (1.0 + gate * (1.0 - sig))).astype(BF)
    dgateup[1] = (dact * silu).astype(BF)
    total[...] = dot(dgateup[0], wgateup[0], NT) + dot(dgateup[1], wgateup[1], NT)
    spread(total, off, own, keep, send)


def mlp_weights(off, both, near, far, near_s, far_s, gains, dgateup, act_low, grads, grad_gateup, grad_down, full):
    gain = gains[1:2, :]
    grad_down[...] = dot(act_low[...], grads[...], TN).astype(BF)
    fill(full, off, both, near, far, near_s, far_s, pick_at(1), lambda b: row_norm(b, gain).astype(BF))
    for c in range(2):
        grad_gateup[c] = dot(full[...], dgateup[c], TN).astype(BF)


def backward_probs(flag, held, fetched, qkv, mixed, probs):
    moved = flag[0] > 0
    for c in range(3):
        qkv[c] = jnp.where(moved, fetched[c], held[c])
    for h in range(2):
        rows = pl.ds(h * HEAD, HEAD)
        probs[h] = probs_of(qkv[1, rows, :], qkv[0, rows, :])
        mixed[rows, :] = dot(qkv[2, rows, :], probs[h].astype(BF), NN).astype(BF)


def backward_attention(
    off, both, near, far, near_s, far_s, qkv, probs, wqkv, wout, dqkv, dmid, own, keep, send, dmixed, total
):
    fill(dmid, off, both, near, far, near_s, far_s, pick_at(None), lambda b: b)
    dmixed[...] = dot(wout[...], dmid[...], NT).astype(BF)
    for h in range(2):
        rows = pl.ds(h * HEAD, HEAD)
        out = dmixed[rows, :]
        weight = probs[h]
        dqkv[2, rows, :] = dot(out, weight.astype(BF), NT).astype(BF)
        dprob = dot(qkv[2, rows, :], out, TN)
        inner = jnp.sum(dprob * weight, axis=0, keepdims=True)
        dscore = (weight * (dprob - inner) * HEAD ** (-0.5)).astype(BF)
        dqkv[0, rows, :] = dot(qkv[1, rows, :], dscore, NN).astype(BF)
        dqkv[1, rows, :] = dot(qkv[0, rows, :], dscore, NT).astype(BF)
    total[...] = dot(dqkv[0], wqkv[0], TN) + dot(dqkv[1], wqkv[1], TN) + dot(dqkv[2], wqkv[2], TN)
    spread(total, off, own, keep, send)


def attention_weights(
    off, both, near, far, near_s, far_s, gains, dqkv, mixed, dmid, wqkv, grad_qkv, grad_out, gain_terms, full
):
    gain = gains[0:1, :]
    grad_out[...] = dot(mixed[...], dmid[...], NN).astype(BF)
    fill(full, off, both, near, far, near_s, far_s, pick_at(0), lambda b: row_norm(b, gain).astype(BF))
    terms = jnp.zeros((1, D), F32)
    for c in range(3):
        grad = dot(dqkv[c], full[...], NN)
        grad_qkv[c] = grad.astype(BF)
        terms += jnp.sum(grad * wqkv[c].astype(F32), axis=0, keepdims=True)
    gain_terms[...] = terms / gain


def norm_step(row, want_terms):
    def body(residual, source, first, second, gains, *outs):
        gain = gains[row : row + 1, :]
        values = source[...].astype(F32)
        inverse = lax.rsqrt(jnp.mean(values * values, axis=-1, keepdims=True) + EPSILON)
        normal = values * inverse
        upstream = first[...] + second[...].astype(F32)
        scaled = upstream * gain
        inner = jnp.mean(scaled * normal, axis=-1, keepdims=True)
        outs[0][...] = (residual[...].astype(F32) + inverse * (scaled - normal * inner)).astype(BF)
        if want_terms:
            outs[1][...] = jnp.sum(upstream * normal, axis=0, keepdims=True)

    return body


def shifted(value, by):
    count = lax.axis_size("section")
    pairs = [(i, i + by) for i in range(count) if 0 <= i + by < count]
    return lax.ppermute(value, "section", pairs)


def mirrored(value):
    count = lax.axis_size("section")
    return lax.ppermute(value, "section", [(i, count - 1 - i) for i in range(count)])


def on_device(
    layer_inputs, output_grads, held_inputs, held_qkv, held_gateup, swapped_pairs,
    w_qkv, w_out, w_gateup, w_down, norm_gains,
):
    sections = lax.axis_size("section")
    position = lax.axis_index("section")
    pair_index = jnp.minimum(position, sections - 1 - position)
    evicted = jnp.sum(jnp.where(jnp.arange(sections // 2) == pair_index, swapped_pairs, 0)) > 0
    flag = evicted.astype(jnp.int32).reshape(1)
    place = lax.axis_index("tensor")
    chip, core = place // 2, place % 2
    step = 2 * core - 1
    off = 32 * jnp.stack(
        [
            ((chip + dz) % 4) * 2 + c
            for dz, c in (
                (0, core), (0, 1 - core), (step, core), (step, 1 - core),
                (2, core), (-step, 1 - core), (-step, core), (2, 1 - core),
            )
        ]
    ).astype(jnp.int32)

    layer_in, dy = layer_inputs[0], output_grads[0]
    wqkv = jnp.swapaxes(w_qkv[0], 1, 2)
    held_q = jnp.swapaxes(held_qkv[0], 1, 2)
    wout, wgateup, wdown, gains = w_out[0], w_gateup[0], w_down[0], norm_gains[0]
    held_x, held_g = held_inputs[0], held_gateup[0]
    mega = 256 * 1536 * 2

    fetched_g = mirrored(held_g)
    fetched_x = mirrored(held_x)
    fetched_q = mirrored(held_q)

    x_blocks = gather(layer_in)
    dy_blocks = gather(dy)
    qkv, *parts = call(
        forward_attention, "forward_attention",
        [shape(3, 192, 256)] + SPREAD,
        [pltpu.VMEM((256, D), BF), pltpu.VMEM((192, 256), BF), pltpu.VMEM((256, D), F32)],
        mega * 900, (off, *x_blocks, gains, wqkv, wout),
    )
    first, second = reduce_blocks(*parts)
    mid = (layer_in.astype(F32) + first + second.astype(F32)).astype(BF)

    dgateup, act_low, grads, *parts = call(
        backward_mlp, "backward_mlp",
        [shape(2, 256, 384), shape(256, 384), shape(256, D)] + SPREAD,
        [pltpu.VMEM((256, D), F32)],
        mega * 1152, (off, flag, *dy_blocks, held_g, fetched_g, wgateup, wdown),
    )
    first, second = reduce_blocks(*parts)
    stash_x = jnp.where(evicted, fetched_x, held_x)
    dmid, mid_terms = call(
        norm_step(1, True), "norm_step_mid", [shape(32, D), shape(1, D, dtype=F32)], [],
        32 * D * 20, (dy, stash_x[1], first, second, gains),
    )

    mid_blocks = gather(mid)
    gateup, *parts = call(
        forward_mlp, "forward_mlp",
        [shape(2, 256, 384)] + SPREAD,
        [pltpu.VMEM((256, D), BF), pltpu.VMEM((256, D), F32)],
        mega * 1152, (off, *mid_blocks, gains, wgateup, wdown),
    )
    first, second = reduce_blocks(*parts)
    layer_out = (mid.astype(F32) + first + second.astype(F32)).astype(BF)
    forward_sent = shifted(layer_out, 1)

    stash_q, mixed, probs = call(
        backward_probs, "backward_probs",
        [shape(3, 192, 256), shape(192, 256), shape(2, 256, 256, dtype=F32)], [],
        mega * 128, (flag, held_q, fetched_q),
    )
    dmid_blocks = gather(dmid)
    dqkv, dmid_full, *parts = call(
        backward_attention, "backward_attention",
        [shape(3, 192, 256), shape(256, D)] + SPREAD,
        [pltpu.VMEM((192, 256), BF), pltpu.VMEM((256, D), F32)],
        mega * 1000, (off, *dmid_blocks, stash_q, probs, wqkv, wout),
    )
    first, second = reduce_blocks(*parts)
    (dinput,) = call(
        norm_step(0, False), "norm_step_in", [shape(32, D)], [],
        32 * D * 20, (dmid, stash_x[0], first, second, gains),
    )
    backward_sent = shifted(dinput, -1)

    stash_blocks = gather(stash_x)
    grad_gateup, grad_down = call(
        mlp_weights, "mlp_weights",
        [shape(2, D, 384), shape(384, D)], [pltpu.VMEM((256, D), BF)],
        mega * 1152, (off, *stash_blocks, gains, dgateup, act_low, grads),
    )
    grad_qkv, grad_out, in_terms = call(
        attention_weights, "attention_weights",
        [shape(3, 192, D), shape(192, D), shape(1, D, dtype=F32)], [pltpu.VMEM((256, D), BF)],
        mega * 768, (off, *stash_blocks, gains, dqkv, mixed, dmid_full, wqkv),
    )
    grad_gains = all_sum(jnp.concatenate([in_terms, mid_terms]))

    new_x = jnp.stack([layer_in, mid])
    stash_inputs = jnp.where(evicted, mirrored(new_x), new_x)
    stash_qkv = jnp.where(evicted, mirrored(qkv), qkv)
    stash_gateup = jnp.where(evicted, mirrored(gateup), gateup)
    return (
        forward_sent[None],
        backward_sent[None],
        stash_inputs[None],
        jnp.swapaxes(stash_qkv, 1, 2)[None],
        stash_gateup[None],
        jnp.swapaxes(grad_qkv, 1, 2)[None],
        grad_out[None],
        grad_gateup[None],
        grad_down[None],
        grad_gains[None],
    )


def solution(mesh):
    in_specs = (
        P("section", "tensor", None),
        P("section", "tensor", None),
        P("section", None, "tensor", None),
        P("section", None, None, "tensor"),
        P("section", None, None, "tensor"),
        P(),
        P("section", None, None, "tensor"),
        P("section", "tensor", None),
        P("section", None, None, "tensor"),
        P("section", "tensor", None),
        P("section", None, None),
    )
    out_specs = (
        P("section", "tensor", None),
        P("section", "tensor", None),
        P("section", None, "tensor", None),
        P("section", None, None, "tensor"),
        P("section", None, None, "tensor"),
        P("section", None, None, "tensor"),
        P("section", "tensor", None),
        P("section", None, None, "tensor"),
        P("section", "tensor", None),
        P("section", None, None),
    )
    return jax.shard_map(
        on_device, mesh=mesh, in_specs=in_specs, out_specs=out_specs, check_vma=False
    )
```

```python
import math

import jax
import jax.numpy as jnp
from jax import lax
from jax.experimental import pallas as pl
from jax.experimental.pallas import tpu as pltpu
from jax.sharding import PartitionSpec as P

D = 1536
HEADS = 16
HEAD = D // HEADS
EPSILON = 1e-05
BF = jnp.bfloat16
F32 = jnp.float32
NN = ((1,), (0,))
NT = ((1,), (1,))
TN = ((0,), (0,))
VMEM = 16 * 2**20


def dot(a, b, dims):
    return lax.dot_general(a, b, (dims, ((), ())), preferred_element_type=F32)


def tensor_pairs(step_even, step_odd):
    return [
        (t, ((t // 2 + (step_odd if t % 2 else step_even)) % 4) * 2 + t % 2) for t in range(8)
    ]


CORE = [(t, t ^ 1) for t in range(8)]
GATHER = tensor_pairs(1, -1)
REDUCE = tensor_pairs(-1, 1)


def over(value, pairs):
    return lax.ppermute(value, "tensor", pairs)


def after(value, *earlier):
    return lax.optimization_barrier((value, *earlier))[0] if earlier else value


def add(one, other):
    return (one.astype(F32) + other.astype(F32)).astype(BF)


def gather(own):
    near_0, other = over(own, GATHER), over(own, CORE)
    near_1, far = over(other, GATHER), over(near_0, GATHER)
    s_1 = over(near_1, CORE)
    return own, other, near_0, near_1, far, over(near_0, CORE), s_1, over(after(far, s_1), CORE)


def reduce_blocks(parts):
    held_2 = add(parts[4], over(parts[7], CORE))
    far = over(held_2, REDUCE)
    held_1 = add(parts[3], over(parts[6], CORE))
    near_1 = over(held_1, REDUCE)
    held_0 = add(add(parts[2], over(parts[5], CORE)), far)
    near_0 = over(held_0, REDUCE)
    other = add(parts[1], near_1)
    return (parts[0], near_0, over(other, CORE)), other


def all_sum(value):
    for pairs in (CORE, [(t, t ^ 2) for t in range(8)], [(t, t ^ 4) for t in range(8)]):
        value = value + over(value, pairs)
    return value


def call(body, name, outs, scratch, flops, args, streamed=()):
    smem, vmem = pl.BlockSpec(memory_space=pltpu.SMEM), pl.BlockSpec(memory_space=pltpu.VMEM)
    hbm = pl.BlockSpec(memory_space=pltpu.HBM)
    args = [
        pltpu.with_memory_space_constraint(a, pltpu.HBM) if i in streamed else a
        for i, a in enumerate(args)
    ]
    moved = sum(a.size * a.dtype.itemsize for a in args)
    moved += sum(math.prod(o.shape) * o.dtype.itemsize for o in outs)
    return pl.pallas_call(
        body,
        name=name,
        out_shape=outs,
        in_specs=[
            hbm if i in streamed else smem if a.dtype == jnp.int32 else vmem
            for i, a in enumerate(args)
        ],
        out_specs=[vmem] * len(outs),
        scratch_shapes=scratch,
        cost_estimate=pl.CostEstimate(flops=flops, bytes_accessed=moved, transcendentals=0),
        compiler_params=pltpu.CompilerParams(vmem_limit_bytes=VMEM),
    )(*args)


def shape(*dims, dtype=BF):
    return jax.ShapeDtypeStruct(dims, dtype)


def block_rows():
    place = lax.axis_index("tensor")
    chip, core = place // 2, place % 2
    step = 2 * core - 1
    where = (
        (0, core), (0, 1 - core), (step, core), (step, 1 - core),
        (2, core), (-step, 1 - core), (-step, core), (2, 1 - core),
    )
    starts = [(((chip + dz + 4) % 4) * 2 + c) * 32 for dz, c in where]
    return [pl.ds(pl.multiple_of(start, 32), 32) for start in starts]


def moved_stash(flags):
    position = lax.axis_index("section")
    return flags[jnp.minimum(position, lax.axis_size("section") - 1 - position)] > 0


def unit_scale(values):
    return lax.rsqrt(jnp.mean(values * values, axis=-1, keepdims=True) + EPSILON)


def row_norm(block, gain):
    values = block.astype(F32)
    return values * unit_scale(values) * gain


def fill(full, rows, blocks, which, change=None):
    for place, block in zip(rows, blocks):
        full[place, :] = block[which] if change is None else change(block[which])


def spread(total, rows, parts, which):
    for place, part in zip(rows, parts):
        part[which] = total[place, :].astype(BF)


SPREAD = [shape(2, 32, D)] * 8


PARTS = ((2, 32, D), (3, 192, 256))
STASH = sum(math.prod(part) for part in PARTS) // 128


def stash_blocks():
    start = 0
    for part, (count, length, width) in enumerate(PARTS):
        for column in range(0, width, 128):
            for index in range(count):
                yield part, index, pl.ds(column, 128), pl.ds(start, length)
                start += length


def pack_stash(parts, packed):
    for part, index, columns, rows in stash_blocks():
        packed[rows, :] = parts[part][index, :, columns]


def pick_stash(moved, packed, kept, outs):
    for part, index, columns, rows in stash_blocks():
        if outs[part] is not None:
            outs[part][index, :, columns] = jnp.where(
                moved, packed[rows, :], kept[part][index, :, columns]
            )


def pack_held(x, q, packed):
    pack_stash((x, q), packed)


def pack_new(x, mids, qkv, packed, pair):
    pair[0] = x[...]
    pair[1] = mids[0]
    pack_stash((pair, qkv), packed)


def stash_out(flags, packed, x, mids, qkv, out_x, out_qkv, pair):
    pair[0] = x[...]
    pair[1] = mids[0]
    pick_stash(moved_stash(flags), packed, (pair, qkv), (out_x, out_qkv))


def stash_out_last(flags, moved, kept, out):
    out[...] = jnp.where(moved_stash(flags), moved[...], kept[...])


def probs_of(keys, queries):
    scores = dot(keys, queries, TN) * HEAD ** (-0.5)
    length = scores.shape[0]
    key = lax.broadcasted_iota(jnp.int32, (length, length), 0)
    query = lax.broadcasted_iota(jnp.int32, (length, length), 1)
    scores = jnp.where(key <= query, scores, -1e30)
    powers = jnp.exp(scores - jnp.max(scores, axis=0, keepdims=True))
    return powers / jnp.sum(powers, axis=0, keepdims=True)


def bring(*refs):
    count = len(refs) // 3
    copies = [
        pltpu.make_async_copy(*each)
        for each in zip(refs[:count], refs[count : 2 * count], refs[2 * count :])
    ]
    for copy in copies:
        copy.start()
    for copy in copies:
        copy.wait()


def forward_attention(gains, wqkv, wout, qkv, full, mixed, total):
    for c in range(3):
        qkv[c] = dot(wqkv[c], full[...], NT).astype(BF)
    for h in range(2):
        rows = pl.ds(h * HEAD, HEAD)
        probs = probs_of(qkv[1, rows, :], qkv[0, rows, :]).astype(BF)
        mixed[rows, :] = dot(qkv[2, rows, :], probs, NN).astype(BF)
    total[...] = dot(mixed[...], wout[...], TN)


def forward_mlp(wgateup, wdown, gateup, full, total):
    for c in range(2):
        gateup[c] = dot(full[...], wgateup[c], NN).astype(BF)
    gate = gateup[0].astype(F32)
    act = (gate * jax.nn.sigmoid(gate) * gateup[1].astype(F32)).astype(BF)
    total[...] = dot(act, wdown[...], NN)


def backward_mlp(stash, wgateup, wdown, dgateup, act_low, grads, total):
    gate = stash[0].astype(F32)
    up = stash[1].astype(F32)
    sig = jax.nn.sigmoid(gate)
    silu = gate * sig
    act_low[...] = (silu * up).astype(BF)
    dact = dot(grads[...], wdown[...], NT)
    dgateup[0] = (dact * up * sig * (1.0 + gate * (1.0 - sig))).astype(BF)
    dgateup[1] = (dact * silu).astype(BF)
    total[...] = dot(dgateup[0], wgateup[0], NT) + dot(dgateup[1], wgateup[1], NT)


def backward_attention(qkv, probs, wqkv, wout, dqkv, dmid, dmixed, total):
    dmixed[...] = dot(wout[...], dmid[...], NT).astype(BF)
    for h in range(2):
        rows = pl.ds(h * HEAD, HEAD)
        out = dmixed[rows, :]
        weight = probs[h]
        dqkv[2, rows, :] = dot(out, weight.astype(BF), NT).astype(BF)
        dprob = dot(qkv[2, rows, :], out, TN)
        inner = jnp.sum(dprob * weight, axis=0, keepdims=True)
        dscore = (weight * (dprob - inner) * HEAD ** (-0.5)).astype(BF)
        dqkv[0, rows, :] = dot(qkv[1, rows, :], dscore, NN).astype(BF)
        dqkv[1, rows, :] = dot(qkv[0, rows, :], dscore, NT).astype(BF)
    total[...] = dot(dqkv[0], wqkv[0], TN) + dot(dqkv[1], wqkv[1], TN) + dot(dqkv[2], wqkv[2], TN)


def first_stage(
    flags, own_b, other, near_0, near_1, far, s_0, s_1, s_2, gains, fetched, wqkv, wout, held, wdown, wgateup,
    qkv, dgateup, act_low, grads, p_0, p_1, p_2, p_3, p_4, p_5, p_6, p_7, full, mixed, total, stash,
):
    parts = (p_0, p_1, p_2, p_3, p_4, p_5, p_6, p_7)
    rows, blocks, gain = block_rows(), (own_b, other, near_0, near_1, far, s_0, s_1, s_2), gains[0:1, :]
    fill(full, rows, blocks, 0, lambda part: row_norm(part, gain).astype(BF))
    forward_attention(gains, wqkv, wout, qkv, full, mixed, total)
    spread(total, rows, parts, 0)
    fill(grads, rows, blocks, 1)
    stash[...] = jnp.where(moved_stash(flags), fetched[...], held[...])
    backward_mlp(stash, wgateup, wdown, dgateup, act_low, grads, total)
    spread(total, rows, parts, 1)


def second_stage(
    own_b, other, near_0, near_1, far, s_0, s_1, s_2, gains, stash_q, probs, wgateup, wdown, wout, wqkv,
    gateup, dqkv, dmid, p_0, p_1, p_2, p_3, p_4, p_5, p_6, p_7, full, dmixed, total,
):
    parts = (p_0, p_1, p_2, p_3, p_4, p_5, p_6, p_7)
    rows, blocks, gain = block_rows(), (own_b, other, near_0, near_1, far, s_0, s_1, s_2), gains[1:2, :]
    fill(full, rows, blocks, 0, lambda part: row_norm(part, gain).astype(BF))
    forward_mlp(wgateup, wdown, gateup, full, total)
    spread(total, rows, parts, 0)
    fill(dmid, rows, blocks, 1)
    backward_attention(stash_q, probs, wqkv, wout, dqkv, dmid, dmixed, total)
    spread(total, rows, parts, 1)


def backward_probs(flags, held, fetched, qkv, mixed, probs):
    pick_stash(moved_stash(flags), fetched, (None, held), (None, qkv))
    for h in range(2):
        rows = pl.ds(h * HEAD, HEAD)
        probs[h] = probs_of(qkv[1, rows, :], qkv[0, rows, :])
        mixed[rows, :] = dot(qkv[2, rows, :], probs[h].astype(BF), NN).astype(BF)


def mlp_weights(own_b, other, near_0, near_1, far, s_0, s_1, s_2, gains, dgateup, act_low, grads, grad_gateup, grad_down, full):
    gain = gains[1:2, :]
    grad_down[...] = dot(act_low[...], grads[...], TN).astype(BF)
    fill(full, block_rows(), (own_b, other, near_0, near_1, far, s_0, s_1, s_2), 3, lambda part: row_norm(part, gain).astype(BF))
    for c in range(2):
        grad_gateup[c] = dot(full[...], dgateup[c], TN).astype(BF)


def attention_weights(
    own_b, other, near_0, near_1, far, s_0, s_1, s_2, gains, dqkv, mixed, dmid, wqkv, grad_qkv, grad_out, gain_terms, full,
):
    gain = gains[0:1, :]
    grad_out[...] = dot(mixed[...], dmid[...], NN).astype(BF)
    fill(full, block_rows(), (own_b, other, near_0, near_1, far, s_0, s_1, s_2), 2, lambda part: row_norm(part, gain).astype(BF))
    terms = jnp.zeros((1, D), F32)
    for c in range(3):
        grad = dot(dqkv[c], full[...], NN)
        grad_qkv[c] = grad.astype(BF)
        terms += jnp.sum(grad * wqkv[c].astype(F32), axis=0, keepdims=True)
    gain_terms[...] = terms / gain


def total_of(own, near, second, which):
    return own[which].astype(F32) + near[which].astype(F32) + second[which].astype(F32)


def norm_back(source, gain, upstream):
    values = source.astype(F32)
    inverse = unit_scale(values)
    normal = values * inverse
    scaled = upstream * gain
    inner = jnp.mean(scaled * normal, axis=-1, keepdims=True)
    return inverse * (scaled - normal * inner), upstream * normal


def middle(flags, held, fetched, x, dy, own, near, second, gains, out, terms, stash):
    pick_stash(moved_stash(flags), fetched, (held, None), (stash, None))
    out[0] = (x[...].astype(F32) + total_of(own, near, second, 0)).astype(BF)
    back, products = norm_back(stash[1], gains[1:2, :], total_of(own, near, second, 1))
    out[1] = (dy[...].astype(F32) + back).astype(BF)
    out[2] = stash[0]
    out[3] = stash[1]
    terms[...] = jnp.sum(products, axis=0, keepdims=True)


def last(mids, own, near, second, gains, layer_out, dinput):
    layer_out[...] = (mids[0].astype(F32) + total_of(own, near, second, 0)).astype(BF)
    back, _ = norm_back(mids[2], gains[0:1, :], total_of(own, near, second, 1))
    dinput[...] = (mids[1].astype(F32) + back).astype(BF)


def shifted(value, by):
    count = lax.axis_size("section")
    pairs = [(i, i + by) for i in range(count) if 0 <= i + by < count]
    return lax.ppermute(value, "section", pairs)


def mirrored(value):
    count = lax.axis_size("section")
    return lax.ppermute(value, "section", [(i, count - 1 - i) for i in range(count)])


def on_device(
    layer_inputs, output_grads, held_inputs, held_qkv, held_gateup, swapped_pairs,
    w_qkv, w_out, w_gateup, w_down, norm_gains,
):
    layer_in, dy = layer_inputs[0], output_grads[0]
    wqkv = jnp.swapaxes(w_qkv[0], 1, 2)
    held_q = jnp.swapaxes(held_qkv[0], 1, 2)
    wout, wgateup, wdown, gains = w_out[0], w_gateup[0], w_down[0], norm_gains[0]
    held_x, held_g = held_inputs[0], held_gateup[0]
    mega = 256 * 1536 * 2
    full, total = pltpu.VMEM((256, D), BF), pltpu.VMEM((256, D), F32)
    per_head, pair = pltpu.VMEM((192, 256), BF), pltpu.VMEM((2, 32, D), BF)

    blocks = gather(jnp.stack([layer_in, dy]))
    fetched_g = mirrored(after(held_g, blocks[3]))
    (packed,) = call(pack_held, "pack_held", [shape(STASH, 128)], [], 1024, (held_x, held_q))
    fetched = mirrored(after(packed, blocks[4]))
    weights = [after(wqkv, blocks[1]), wout, held_g, wdown, wgateup]
    wqkv, wout, held_g, wdown, wgateup = call(
        bring, "bring", [pltpu.VMEM(w.shape, w.dtype) for w in weights],
        [pltpu.SemaphoreType.DMA(()) for _ in weights], 0, weights, (0, 1, 2, 3, 4),
    )

    qkv, dgateup, act_low, grads, *parts = call(
        first_stage, "first_stage",
        [shape(3, 192, 256), shape(2, 256, 384), shape(256, 384), shape(256, D)] + SPREAD,
        [full, per_head, total, pltpu.VMEM((2, 256, 384), BF)],
        mega * 2050,
        (swapped_pairs, *blocks, gains, fetched_g, wqkv, wout, held_g, wdown, wgateup),
    )
    parts[7] = after(parts[7], fetched)
    sums, _ = reduce_blocks(parts)
    mids, mid_terms = call(
        middle, "middle", [shape(4, 32, D), shape(1, D, dtype=F32)], [pair],
        32 * D * 40, (swapped_pairs, held_x, fetched, layer_in, dy, *sums, gains),
    )

    stash_q, mixed, probs = call(
        backward_probs, "backward_probs",
        [shape(3, 192, 256), shape(192, 256), shape(2, 256, 256, dtype=F32)], [],
        mega * 128, (swapped_pairs, held_q, fetched),
    )
    blocks = gather(mids)
    (packed,) = call(pack_new, "pack_new", [shape(STASH, 128)], [pair], 1024, (layer_in, mids, qkv))
    moved = mirrored(after(packed, blocks[2]))

    gateup, dqkv, dmid, *parts = call(
        second_stage, "second_stage",
        [shape(2, 256, 384), shape(3, 192, 256), shape(256, D)] + SPREAD,
        [full, per_head, total],
        mega * 2150,
        (*blocks, gains, stash_q, probs, wgateup, wdown, wout, wqkv),
    )
    parts[7] = after(parts[7], moved)
    sums, other = reduce_blocks(parts)
    moved_gateup = mirrored(after(gateup, other))

    grad_qkv, grad_out, in_terms = call(
        attention_weights, "attention_weights",
        [shape(3, 192, D), shape(192, D), shape(1, D, dtype=F32)], [full],
        mega * 768, (*blocks, gains, dqkv, mixed, dmid, wqkv),
    )
    grad_gateup, grad_down = call(
        mlp_weights, "mlp_weights",
        [shape(2, D, 384), shape(384, D)], [full],
        mega * 1152, (*blocks, gains, dgateup, act_low, after(grads, gateup)),
    )
    layer_out, dinput = call(
        last, "last", [shape(32, D), shape(32, D)], [],
        32 * D * 40, (after(mids, grad_down, in_terms), *sums, gains),
    )
    forward_sent = shifted(layer_out, 1)
    backward_sent = shifted(dinput, -1)
    grad_gains = all_sum(jnp.concatenate([in_terms, mid_terms]))

    stash_inputs, stash_qkv = call(
        stash_out, "stash_out", [shape(*part) for part in PARTS], [pair],
        1024, (swapped_pairs, moved, layer_in, mids, qkv),
    )
    (stash_gateup,) = call(
        stash_out_last, "stash_out_last", [shape(2, 256, 384)], [],
        1024, (swapped_pairs, moved_gateup, gateup),
    )
    return (
        forward_sent[None],
        backward_sent[None],
        stash_inputs[None],
        jnp.swapaxes(stash_qkv, 1, 2)[None],
        stash_gateup[None],
        jnp.swapaxes(grad_qkv, 1, 2)[None],
        grad_out[None],
        grad_gateup[None],
        grad_down[None],
        grad_gains[None],
    )


def solution(mesh):
    in_specs = (
        P("section", "tensor", None),
        P("section", "tensor", None),
        P("section", None, "tensor", None),
        P("section", None, None, "tensor"),
        P("section", None, None, "tensor"),
        P(),
        P("section", None, None, "tensor"),
        P("section", "tensor", None),
        P("section", None, None, "tensor"),
        P("section", "tensor", None),
        P("section", None, None),
    )
    out_specs = (
        P("section", "tensor", None),
        P("section", "tensor", None),
        P("section", None, "tensor", None),
        P("section", None, None, "tensor"),
        P("section", None, None, "tensor"),
        P("section", None, None, "tensor"),
        P("section", "tensor", None),
        P("section", None, None, "tensor"),
        P("section", "tensor", None),
        P("section", None, None),
    )
    return jax.shard_map(
        on_device, mesh=mesh, in_specs=in_specs, out_specs=out_specs, check_vma=False
    )
```

```python
import math

import jax
import jax.numpy as jnp
from jax import lax
from jax.experimental import pallas as pl
from jax.experimental.pallas import tpu as pltpu
from jax.sharding import PartitionSpec as P

D = 1536
HEADS = 16
HEAD = D // HEADS
EPSILON = 1e-05
BF = jnp.bfloat16
F32 = jnp.float32
NN = ((1,), (0,))
NT = ((1,), (1,))
TN = ((0,), (0,))
VMEM = 16 * 2**20


def dot(a, b, dims):
    return lax.dot_general(a, b, (dims, ((), ())), preferred_element_type=F32)


def tensor_pairs(step_even, step_odd):
    return [
        (t, ((t // 2 + (step_odd if t % 2 else step_even)) % 4) * 2 + t % 2) for t in range(8)
    ]


CORE = [(t, t ^ 1) for t in range(8)]
GATHER = tensor_pairs(1, -1)
REDUCE = tensor_pairs(-1, 1)


def over(value, pairs):
    return lax.ppermute(value, "tensor", pairs)


def after(value, *earlier):
    return lax.optimization_barrier((value, *earlier))[0] if earlier else value


def add(one, other):
    return (one.astype(F32) + other.astype(F32)).astype(BF)


def gather(own, before_far=(), before_s0=lambda near_0: ()):
    near_0, other = over(own, GATHER), over(own, CORE)
    near_1, far = over(other, GATHER), over(after(near_0, *before_far), GATHER)
    s_1 = over(near_1, CORE)
    return own, other, near_0, near_1, far, over(after(near_0, *before_s0(near_0)), CORE), s_1, over(after(far, s_1), CORE)


def start_sums(parts, *before_near):
    held_2 = add(parts[4], over(parts[7], CORE))
    far = over(held_2, REDUCE)
    held_1 = add(parts[3], over(after(parts[6], held_2, *before_near), CORE))
    return held_2, held_1, far, add(parts[1], over(held_1, REDUCE))


def last_held(parts, far):
    return add(add(parts[2], over(parts[5], CORE)), far)


def end_sums(parts, held_0, other):
    return parts[0], over(held_0, REDUCE), over(other, CORE)


def add_across(value, bit):
    return value + over(value, [(t, t ^ bit) for t in range(8)])


def call(body, name, outs, scratch, flops, args, streamed=()):
    smem, vmem = pl.BlockSpec(memory_space=pltpu.SMEM), pl.BlockSpec(memory_space=pltpu.VMEM)
    hbm = pl.BlockSpec(memory_space=pltpu.HBM)
    args = [
        pltpu.with_memory_space_constraint(a, pltpu.HBM) if i in streamed else a
        for i, a in enumerate(args)
    ]
    moved = 0 if flops < 4096 else sum(a.size * a.dtype.itemsize for a in args)
    moved += 1024 if flops < 4096 else sum(math.prod(o.shape) * o.dtype.itemsize for o in outs)
    return pl.pallas_call(
        body,
        name=name,
        out_shape=outs,
        in_specs=[
            hbm if i in streamed else smem if a.dtype == jnp.int32 else vmem
            for i, a in enumerate(args)
        ],
        out_specs=[vmem] * len(outs),
        scratch_shapes=scratch,
        cost_estimate=pl.CostEstimate(flops=flops, bytes_accessed=moved, transcendentals=0),
        compiler_params=pltpu.CompilerParams(vmem_limit_bytes=VMEM),
    )(*args)


def shape(*dims, dtype=BF):
    return jax.ShapeDtypeStruct(dims, dtype)


def block_rows():
    place = lax.axis_index("tensor")
    chip, core = place // 2, place % 2
    step = 2 * core - 1
    where = (
        (0, core), (0, 1 - core), (step, core), (step, 1 - core),
        (2, core), (-step, 1 - core), (-step, core), (2, 1 - core),
    )
    starts = [(((chip + dz + 4) % 4) * 2 + c) * 32 for dz, c in where]
    return [pl.ds(pl.multiple_of(start, 32), 32) for start in starts]


def moved_stash(flags):
    position = lax.axis_index("section")
    return flags[jnp.minimum(position, lax.axis_size("section") - 1 - position)] > 0


def unit_scale(values):
    return lax.rsqrt(jnp.mean(values * values, axis=-1, keepdims=True) + EPSILON)


def row_norm(block, gain):
    values = block.astype(F32)
    return values * unit_scale(values) * gain


def fill(full, rows, blocks, which, change=None):
    for place, block in zip(rows, blocks):
        full[place, :] = block[which] if change is None else change(block[which])


def spread(total, rows, parts, which):
    for place, part in zip(rows, parts):
        part[which] = total[place, :].astype(BF)


SPREAD = [shape(2, 32, D)] * 8


PARTS = ((2, 32, D), (3, 192, 256))
STASH = sum(math.prod(part) for part in PARTS) // 128


def stash_blocks():
    start = 0
    for part, (count, length, width) in enumerate(PARTS):
        for column in range(0, width, 128):
            for index in range(count):
                yield part, index, pl.ds(column, 128), pl.ds(start, length)
                start += length


def pack_stash(parts, packed):
    for part, index, columns, rows in stash_blocks():
        packed[rows, :] = parts[part][index, :, columns]


def pick_stash(moved, packed, kept, outs):
    for part, index, columns, rows in stash_blocks():
        if outs[part] is not None:
            outs[part][index, :, columns] = jnp.where(
                moved, packed[rows, :], kept[part][index, :, columns]
            )


def pack_held(x, q, packed):
    pack_stash((x, q), packed)


def pack_new(x, mids, qkv, packed, pair):
    pair[0] = x[...]
    pair[1] = mids[0]
    pack_stash((pair, qkv), packed)


def stash_out(flags, packed, x, mids, qkv, out_x, out_qkv, pair):
    pair[0] = x[...]
    pair[1] = mids[0]
    pick_stash(moved_stash(flags), packed, (pair, qkv), (out_x, out_qkv))


def stash_out_last(flags, moved, kept, out):
    out[...] = jnp.where(moved_stash(flags), moved[...], kept[...])


def probs_of(keys, queries):
    scores = dot(keys, queries, TN) * HEAD ** (-0.5)
    length = scores.shape[0]
    key = lax.broadcasted_iota(jnp.int32, (length, length), 0)
    query = lax.broadcasted_iota(jnp.int32, (length, length), 1)
    scores = jnp.where(key <= query, scores, -1e30)
    powers = jnp.exp(scores - jnp.max(scores, axis=0, keepdims=True))
    return powers / jnp.sum(powers, axis=0, keepdims=True)


def copy_all(copies):
    copies = [pltpu.make_async_copy(*each) for each in copies]
    for copy in copies:
        copy.start()
    for copy in copies:
        copy.wait()


def bring(*refs):
    count = len(refs) // 3
    copy_all(zip(refs[:count], refs[count : 2 * count], refs[2 * count :]))


def stack(one, other, out, first, second):
    copy_all(((one, out.at[0], first), (other, out.at[1], second)))


def forward_attention(gains, wqkv, wout, qkv, full, mixed, total):
    for c in range(3):
        qkv[c] = dot(wqkv[c], full[...], NT).astype(BF)
    for h in range(2):
        rows = pl.ds(h * HEAD, HEAD)
        probs = probs_of(qkv[1, rows, :], qkv[0, rows, :]).astype(BF)
        mixed[rows, :] = dot(qkv[2, rows, :], probs, NN).astype(BF)
    total[...] = dot(mixed[...], wout[...], TN)


def forward_mlp(wgateup, wdown, gateup, full, total):
    for c in range(2):
        gateup[c] = dot(full[...], wgateup[c], NN).astype(BF)
    gate = gateup[0].astype(F32)
    act = (gate * jax.nn.sigmoid(gate) * gateup[1].astype(F32)).astype(BF)
    total[...] = dot(act, wdown[...], NN)


def backward_mlp(stash, wgateup, wdown, dgateup, act_low, grads, total):
    gate = stash[0].astype(F32)
    up = stash[1].astype(F32)
    sig = jax.nn.sigmoid(gate)
    silu = gate * sig
    act_low[...] = (silu * up).astype(BF)
    dact = dot(grads[...], wdown[...], NT)
    dgateup[0] = (dact * up * sig * (1.0 + gate * (1.0 - sig))).astype(BF)
    dgateup[1] = (dact * silu).astype(BF)
    total[...] = dot(dgateup[0], wgateup[0], NT) + dot(dgateup[1], wgateup[1], NT)


def backward_attention(qkv, probs, wqkv, wout, dqkv, dmid, dmixed, total):
    dmixed[...] = dot(wout[...], dmid[...], NT).astype(BF)
    for h in range(2):
        rows = pl.ds(h * HEAD, HEAD)
        out = dmixed[rows, :]
        weight = probs[h]
        dqkv[2, rows, :] = dot(out, weight.astype(BF), NT).astype(BF)
        dprob = dot(qkv[2, rows, :], out, TN)
        inner = jnp.sum(dprob * weight, axis=0, keepdims=True)
        dscore = (weight * (dprob - inner) * HEAD ** (-0.5)).astype(BF)
        dqkv[0, rows, :] = dot(qkv[1, rows, :], dscore, NN).astype(BF)
        dqkv[1, rows, :] = dot(qkv[0, rows, :], dscore, NT).astype(BF)
    total[...] = dot(dqkv[0], wqkv[0], TN) + dot(dqkv[1], wqkv[1], TN) + dot(dqkv[2], wqkv[2], TN)


def first_stage(
    flags, own_b, other, near_0, near_1, far, s_0, s_1, s_2, gains, fetched, wqkv, wout, held, wdown, wgateup,
    qkv, dgateup, act_low, grads, p_0, p_1, p_2, p_3, p_4, p_5, p_6, p_7, full, mixed, total, stash,
):
    parts = (p_0, p_1, p_2, p_3, p_4, p_5, p_6, p_7)
    rows, blocks, gain = block_rows(), (own_b, other, near_0, near_1, far, s_0, s_1, s_2), gains[0:1, :]
    fill(full, rows, blocks, 0, lambda part: row_norm(part, gain).astype(BF))
    forward_attention(gains, wqkv, wout, qkv, full, mixed, total)
    spread(total, rows, parts, 0)
    fill(grads, rows, blocks, 1)
    stash[...] = jnp.where(moved_stash(flags), fetched[...], held[...])
    backward_mlp(stash, wgateup, wdown, dgateup, act_low, grads, total)
    spread(total, rows, parts, 1)


def second_stage(
    own_b, other, near_0, near_1, far, s_0, s_1, s_2, gains, stash_q, probs, wgateup, wdown, wout, wqkv,
    gateup, dqkv, dmid, p_0, p_1, p_2, p_3, p_4, p_5, p_6, p_7, full, dmixed, total,
):
    parts = (p_0, p_1, p_2, p_3, p_4, p_5, p_6, p_7)
    rows, blocks, gain = block_rows(), (own_b, other, near_0, near_1, far, s_0, s_1, s_2), gains[1:2, :]
    fill(full, rows, blocks, 0, lambda part: row_norm(part, gain).astype(BF))
    forward_mlp(wgateup, wdown, gateup, full, total)
    spread(total, rows, parts, 0)
    fill(dmid, rows, blocks, 1)
    backward_attention(stash_q, probs, wqkv, wout, dqkv, dmid, dmixed, total)
    spread(total, rows, parts, 1)


def backward_probs(flags, held, fetched, qkv, mixed, probs):
    pick_stash(moved_stash(flags), fetched, (None, held), (None, qkv))
    for h in range(2):
        rows = pl.ds(h * HEAD, HEAD)
        probs[h] = probs_of(qkv[1, rows, :], qkv[0, rows, :])
        mixed[rows, :] = dot(qkv[2, rows, :], probs[h].astype(BF), NN).astype(BF)


def mlp_weights(own_b, other, near_0, near_1, far, s_0, s_1, s_2, gains, dgateup, act_low, grads, grad_gateup, grad_down, full):
    gain = gains[1:2, :]
    grad_down[...] = dot(act_low[...], grads[...], TN).astype(BF)
    fill(full, block_rows(), (own_b, other, near_0, near_1, far, s_0, s_1, s_2), 3, lambda part: row_norm(part, gain).astype(BF))
    for c in range(2):
        grad_gateup[c] = dot(full[...], dgateup[c], TN).astype(BF)


def attention_weights(
    own_b, other, near_0, near_1, far, s_0, s_1, s_2, gains, dqkv, mixed, dmid, wqkv, grad_qkv, grad_out, gain_terms, full,
):
    gain = gains[0:1, :]
    grad_out[...] = dot(mixed[...], dmid[...], NN).astype(BF)
    fill(full, block_rows(), (own_b, other, near_0, near_1, far, s_0, s_1, s_2), 2, lambda part: row_norm(part, gain).astype(BF))
    terms = jnp.zeros((1, D), F32)
    for c in range(3):
        grad = dot(dqkv[c], full[...], NN)
        grad_qkv[c] = grad.astype(BF)
        terms += jnp.sum(grad * wqkv[c].astype(F32), axis=0, keepdims=True)
    gain_terms[...] = terms / gain


def total_of(own, near, second, which):
    return own[which].astype(F32) + near[which].astype(F32) + second[which].astype(F32)


def norm_back(source, gain, upstream):
    values = source.astype(F32)
    inverse = unit_scale(values)
    normal = values * inverse
    scaled = upstream * gain
    inner = jnp.mean(scaled * normal, axis=-1, keepdims=True)
    return inverse * (scaled - normal * inner), upstream * normal


def middle(flags, held, fetched, x, dy, own, near, second, gains, out, terms, stash):
    pick_stash(moved_stash(flags), fetched, (held, None), (stash, None))
    out[0] = (x[...].astype(F32) + total_of(own, near, second, 0)).astype(BF)
    back, products = norm_back(stash[1], gains[1:2, :], total_of(own, near, second, 1))
    out[1] = (dy[...].astype(F32) + back).astype(BF)
    out[2] = stash[0]
    out[3] = stash[1]
    terms[...] = jnp.sum(products, axis=0, keepdims=True)


def last(mids, own, near, second, gains, layer_out, dinput):
    layer_out[...] = (mids[0].astype(F32) + total_of(own, near, second, 0)).astype(BF)
    back, _ = norm_back(mids[2], gains[0:1, :], total_of(own, near, second, 1))
    dinput[...] = (mids[1].astype(F32) + back).astype(BF)


def shifted(value, by):
    count = lax.axis_size("section")
    pairs = [(i, i + by) for i in range(count) if 0 <= i + by < count]
    return lax.ppermute(value, "section", pairs)


def mirrored(value):
    count = lax.axis_size("section")
    return lax.ppermute(value, "section", [(i, count - 1 - i) for i in range(count)])


def on_device(
    layer_inputs, output_grads, held_inputs, held_qkv, held_gateup, swapped_pairs,
    w_qkv, w_out, w_gateup, w_down, norm_gains,
):
    layer_in, dy = layer_inputs[0], output_grads[0]
    wqkv = jnp.swapaxes(w_qkv[0], 1, 2)
    held_q = jnp.swapaxes(held_qkv[0], 1, 2)
    wout, wgateup, wdown, gains = w_out[0], w_gateup[0], w_down[0], norm_gains[0]
    held_x, held_g = held_inputs[0], held_gateup[0]
    mega = 256 * 1536 * 2
    full, total = pltpu.VMEM((256, D), BF), pltpu.VMEM((256, D), F32)
    per_head, pair = pltpu.VMEM((192, 256), BF), pltpu.VMEM((2, 32, D), BF)

    own = call(
        stack, "stack", [shape(2, 32, D)], [pltpu.SemaphoreType.DMA(())] * 2, 8192, (layer_in, dy), (0, 1)
    )[0]
    fetched_g = mirrored(after(held_g, own))
    weights = [after(wqkv, own), wout, held_g, wdown, wgateup]
    wqkv, wout, held_g, wdown, wgateup = call(
        bring, "bring", [pltpu.VMEM(w.shape, w.dtype) for w in weights],
        [pltpu.SemaphoreType.DMA(()) for _ in weights], 8192, weights, (0, 1, 2, 3, 4),
    )
    (packed,) = call(pack_held, "pack_held", [shape(STASH, 128)], [], 8192, (held_x, after(held_q, own)))
    blocks = gather(own, (wqkv, packed), lambda _: (fetched_g,))
    fetched = mirrored(after(packed, blocks[4]))

    qkv, dgateup, act_low, grads, *parts = call(
        first_stage, "first_stage",
        [shape(3, 192, 256), shape(2, 256, 384), shape(256, 384), shape(256, D)] + SPREAD,
        [full, per_head, total, pltpu.VMEM((2, 256, 384), BF)],
        mega * 2050,
        (swapped_pairs, *blocks, gains, fetched_g, wqkv, wout, held_g, wdown, wgateup),
    )
    parts[7] = after(parts[7], fetched)
    _, _, far, other = start_sums(parts)
    sums = end_sums(parts, last_held(parts, far), other)
    mids, mid_terms = call(
        middle, "middle", [shape(4, 32, D), shape(1, D, dtype=F32)], [pair],
        32 * D * 40, (swapped_pairs, held_x, fetched, layer_in, dy, *sums, gains),
    )

    stash_q, mixed, probs = call(
        backward_probs, "backward_probs",
        [shape(3, 192, 256), shape(192, 256), shape(2, 256, 256, dtype=F32)], [],
        1024, (swapped_pairs, held_q, fetched),
    )
    blocks = gather(mids, (probs,))
    (packed,) = call(pack_new, "pack_new", [shape(STASH, 128)], [pair], 1024, (layer_in, mids, qkv))
    moved = mirrored(after(packed, blocks[2]))

    gateup, dqkv, dmid, *parts = call(
        second_stage, "second_stage",
        [shape(2, 256, 384), shape(3, 192, 256), shape(256, D)] + SPREAD,
        [full, per_head, total],
        1024,
        (*blocks, gains, stash_q, probs, wgateup, wdown, wout, wqkv),
    )

    grad_qkv, grad_out, in_terms = call(
        attention_weights, "attention_weights",
        [shape(3, 192, D), shape(192, D), shape(1, D, dtype=F32)], [full],
        1024, (*blocks, gains, dqkv, mixed, dmid, wqkv),
    )
    grad_gateup, grad_down = call(
        mlp_weights, "mlp_weights",
        [shape(2, D, 384), shape(384, D)], [full],
        1024, (*blocks, gains, dgateup, act_low, after(grads, gateup)),
    )
    parts[7] = after(parts[7], moved, in_terms, grad_down)
    held_2, held_1, far, other = start_sums(parts)
    moved_gateup = mirrored(after(gateup, other))
    terms = add_across(jnp.concatenate([in_terms, mid_terms]), 1)
    terms = add_across(after(terms, held_2), 2)
    stash_inputs, stash_qkv = call(
        stash_out, "stash_out", [shape(*part) for part in PARTS], [pair],
        1024, (swapped_pairs, after(moved, held_2), layer_in, mids, qkv),
    )
    held_0 = after(last_held(parts, far), terms, stash_inputs)
    grad_gains = add_across(after(terms, held_0), 4)
    sums = end_sums(parts, held_0, other)
    layer_out, dinput = call(
        last, "last", [shape(32, D), shape(32, D)], [],
        32 * D * 40, (mids, *sums, gains),
    )
    forward_sent = shifted(layer_out, 1)
    backward_sent = shifted(dinput, -1)
    (stash_gateup,) = call(
        stash_out_last, "stash_out_last", [shape(2, 256, 384)], [],
        1024, (swapped_pairs, moved_gateup, gateup),
    )

    return (
        forward_sent[None],
        backward_sent[None],
        stash_inputs[None],
        jnp.swapaxes(stash_qkv, 1, 2)[None],
        stash_gateup[None],
        jnp.swapaxes(grad_qkv, 1, 2)[None],
        grad_out[None],
        grad_gateup[None],
        grad_down[None],
        grad_gains[None],
    )


def solution(mesh):
    in_specs = (
        P("section", "tensor", None),
        P("section", "tensor", None),
        P("section", None, "tensor", None),
        P("section", None, None, "tensor"),
        P("section", None, None, "tensor"),
        P(),
        P("section", None, None, "tensor"),
        P("section", "tensor", None),
        P("section", None, None, "tensor"),
        P("section", "tensor", None),
        P("section", None, None),
    )
    out_specs = (
        P("section", "tensor", None),
        P("section", "tensor", None),
        P("section", None, "tensor", None),
        P("section", None, None, "tensor"),
        P("section", None, None, "tensor"),
        P("section", None, None, "tensor"),
        P("section", "tensor", None),
        P("section", None, None, "tensor"),
        P("section", "tensor", None),
        P("section", None, None),
    )
    return jax.shard_map(
        on_device, mesh=mesh, in_specs=in_specs, out_specs=out_specs, check_vma=False
    )
```

```python
import math

import jax
import jax.numpy as jnp
from jax import lax
from jax.experimental import pallas as pl
from jax.experimental.pallas import tpu as pltpu
from jax.sharding import PartitionSpec as P

D = 1536
HEADS = 16
HEAD = D // HEADS
EPSILON = 1e-05
BF = jnp.bfloat16
F32 = jnp.float32
NN = ((1,), (0,))
NT = ((1,), (1,))
TN = ((0,), (0,))
VMEM = 16 * 2**20


def dot(a, b, dims):
    return lax.dot_general(a, b, (dims, ((), ())), preferred_element_type=F32)


def tensor_pairs(step_even, step_odd):
    return [
        (t, ((t // 2 + (step_odd if t % 2 else step_even)) % 4) * 2 + t % 2) for t in range(8)
    ]


CORE = [(t, t ^ 1) for t in range(8)]
GATHER = tensor_pairs(1, -1)
REDUCE = tensor_pairs(-1, 1)


def over(value, pairs):
    return lax.ppermute(value, "tensor", pairs)


def after(value, *earlier):
    return lax.optimization_barrier((value, *earlier))[0] if earlier else value


def add(one, other):
    return (one.astype(F32) + other.astype(F32)).astype(BF)


def gather(own, before_far=(), before_s0=lambda near_0: ()):
    near_0, other = over(own, GATHER), over(own, CORE)
    near_1, far = over(other, GATHER), over(after(near_0, *before_far), GATHER)
    s_1 = over(near_1, CORE)
    return own, other, near_0, near_1, far, over(after(near_0, *before_s0(near_0)), CORE), s_1, over(after(far, s_1), CORE)


def start_sums(parts, *before_near):
    held_2 = add(parts[4], over(parts[7], CORE))
    far = over(held_2, REDUCE)
    held_1 = add(parts[3], over(after(parts[6], held_2, *before_near), CORE))
    return held_2, held_1, far, add(parts[1], over(held_1, REDUCE))


def last_held(parts, far):
    return add(add(parts[2], over(parts[5], CORE)), far)


def end_sums(parts, held_0, other):
    return parts[0], over(held_0, REDUCE), over(other, CORE)


def add_across(value, bit):
    return value + over(value, [(t, t ^ bit) for t in range(8)])


def call(body, name, outs, scratch, flops, args, streamed=()):
    smem, vmem = pl.BlockSpec(memory_space=pltpu.SMEM), pl.BlockSpec(memory_space=pltpu.VMEM)
    hbm = pl.BlockSpec(memory_space=pltpu.HBM)
    args = [
        pltpu.with_memory_space_constraint(a, pltpu.HBM) if i in streamed else a
        for i, a in enumerate(args)
    ]
    moved = 0 if flops < 4096 else sum(a.size * a.dtype.itemsize for a in args)
    moved += 1024 if flops < 4096 else sum(math.prod(o.shape) * o.dtype.itemsize for o in outs)
    return pl.pallas_call(
        body,
        name=name,
        out_shape=outs,
        in_specs=[
            hbm if i in streamed else smem if a.dtype == jnp.int32 else vmem
            for i, a in enumerate(args)
        ],
        out_specs=[vmem] * len(outs),
        scratch_shapes=scratch,
        cost_estimate=pl.CostEstimate(flops=flops, bytes_accessed=moved, transcendentals=0),
        compiler_params=pltpu.CompilerParams(vmem_limit_bytes=VMEM),
    )(*args)


def shape(*dims, dtype=BF):
    return jax.ShapeDtypeStruct(dims, dtype)


def block_rows():
    place = lax.axis_index("tensor")
    chip, core = place // 2, place % 2
    step = 2 * core - 1
    where = (
        (0, core), (0, 1 - core), (step, core), (step, 1 - core),
        (2, core), (-step, 1 - core), (-step, core), (2, 1 - core),
    )
    starts = [(((chip + dz + 4) % 4) * 2 + c) * 32 for dz, c in where]
    return [pl.ds(pl.multiple_of(start, 32), 32) for start in starts]


def moved_stash(flags):
    position = lax.axis_index("section")
    return flags[jnp.minimum(position, lax.axis_size("section") - 1 - position)] > 0


def unit_scale(values):
    return lax.rsqrt(jnp.mean(values * values, axis=-1, keepdims=True) + EPSILON)


def row_norm(block, gain):
    values = block.astype(F32)
    return values * unit_scale(values) * gain


def fill(full, rows, blocks, which, change=None):
    for place, block in zip(rows, blocks):
        full[place, :] = block[which] if change is None else change(block[which])


def spread(total, rows, parts, which):
    for place, part in zip(rows, parts):
        part[which] = total[place, :].astype(BF)


SPREAD = [shape(2, 32, D)] * 8


PARTS = ((2, 32, D), (3, 192, 256))
STASH = sum(math.prod(part) for part in PARTS) // 128


def stash_blocks():
    start = 0
    for part, (count, length, width) in enumerate(PARTS):
        for column in range(0, width, 128):
            for index in range(count):
                yield part, index, pl.ds(column, 128), pl.ds(start, length)
                start += length


def pack_stash(parts, packed):
    for part, index, columns, rows in stash_blocks():
        packed[rows, :] = parts[part][index, :, columns]


def pick_stash(moved, packed, kept, outs):
    for part, index, columns, rows in stash_blocks():
        if outs[part] is not None:
            outs[part][index, :, columns] = jnp.where(
                moved, packed[rows, :], kept[part][index, :, columns]
            )


def pack_held(x, q, packed):
    pack_stash((x, q), packed)


def pack_new(x, mids, qkv, packed, pair):
    pair[0] = x[...]
    pair[1] = mids[0]
    pack_stash((pair, qkv), packed)


def stash_out(flags, packed, x, mids, qkv, out_x, out_qkv, pair):
    pair[0] = x[...]
    pair[1] = mids[0]
    pick_stash(moved_stash(flags), packed, (pair, qkv), (out_x, out_qkv))


def stash_out_last(flags, moved, kept, out):
    out[...] = jnp.where(moved_stash(flags), moved[...], kept[...])


def probs_of(keys, queries):
    scores = dot(keys, queries, TN) * HEAD ** (-0.5)
    length = scores.shape[0]
    key = lax.broadcasted_iota(jnp.int32, (length, length), 0)
    query = lax.broadcasted_iota(jnp.int32, (length, length), 1)
    scores = jnp.where(key <= query, scores, -1e30)
    powers = jnp.exp(scores - jnp.max(scores, axis=0, keepdims=True))
    return powers / jnp.sum(powers, axis=0, keepdims=True)


def copy_all(copies):
    copies = [pltpu.make_async_copy(*each) for each in copies]
    for copy in copies:
        copy.start()
    for copy in copies:
        copy.wait()


def bring(*refs):
    count = len(refs) // 3
    copy_all(zip(refs[:count], refs[count : 2 * count], refs[2 * count :]))


def stack(one, other, out, first, second):
    copy_all(((one, out.at[0], first), (other, out.at[1], second)))


def forward_attention(gains, wqkv, wout, qkv, full, mixed, total):
    for c in range(3):
        qkv[c] = dot(wqkv[c], full[...], NT).astype(BF)
    for h in range(2):
        rows = pl.ds(h * HEAD, HEAD)
        probs = probs_of(qkv[1, rows, :], qkv[0, rows, :]).astype(BF)
        mixed[rows, :] = dot(qkv[2, rows, :], probs, NN).astype(BF)
    total[...] = dot(mixed[...], wout[...], TN)


def forward_mlp(wgateup, wdown, gateup, full, total):
    for c in range(2):
        gateup[c] = dot(full[...], wgateup[c], NN).astype(BF)
    gate = gateup[0].astype(F32)
    act = (gate * jax.nn.sigmoid(gate) * gateup[1].astype(F32)).astype(BF)
    total[...] = dot(act, wdown[...], NN)


def backward_mlp(stash, wgateup, wdown, dgateup, act_low, grads, total):
    gate = stash[0].astype(F32)
    up = stash[1].astype(F32)
    sig = jax.nn.sigmoid(gate)
    silu = gate * sig
    act_low[...] = (silu * up).astype(BF)
    dact = dot(grads[...], wdown[...], NT)
    dgateup[0] = (dact * up * sig * (1.0 + gate * (1.0 - sig))).astype(BF)
    dgateup[1] = (dact * silu).astype(BF)
    total[...] = dot(dgateup[0], wgateup[0], NT) + dot(dgateup[1], wgateup[1], NT)


def backward_attention(qkv, probs, wqkv, wout, dqkv, dmid, dmixed, total):
    dmixed[...] = dot(wout[...], dmid[...], NT).astype(BF)
    for h in range(2):
        rows = pl.ds(h * HEAD, HEAD)
        out = dmixed[rows, :]
        weight = probs[h]
        dqkv[2, rows, :] = dot(out, weight.astype(BF), NT).astype(BF)
        dprob = dot(qkv[2, rows, :], out, TN)
        inner = jnp.sum(dprob * weight, axis=0, keepdims=True)
        dscore = (weight * (dprob - inner) * HEAD ** (-0.5)).astype(BF)
        dqkv[0, rows, :] = dot(qkv[1, rows, :], dscore, NN).astype(BF)
        dqkv[1, rows, :] = dot(qkv[0, rows, :], dscore, NT).astype(BF)
    total[...] = dot(dqkv[0], wqkv[0], TN) + dot(dqkv[1], wqkv[1], TN) + dot(dqkv[2], wqkv[2], TN)


def first_stage(
    flags, own_b, other, near_0, near_1, far, s_0, s_1, s_2, gains, fetched, wqkv, wout, held, wdown, wgateup,
    qkv, dgateup, act_low, grads, p_0, p_1, p_2, p_3, p_4, p_5, p_6, p_7, full, mixed, total, stash,
):
    parts = (p_0, p_1, p_2, p_3, p_4, p_5, p_6, p_7)
    rows, blocks, gain = block_rows(), (own_b, other, near_0, near_1, far, s_0, s_1, s_2), gains[0:1, :]
    fill(full, rows, blocks, 0, lambda part: row_norm(part, gain).astype(BF))
    forward_attention(gains, wqkv, wout, qkv, full, mixed, total)
    spread(total, rows, parts, 0)
    fill(grads, rows, blocks, 1)
    stash[...] = jnp.where(moved_stash(flags), fetched[...], held[...])
    backward_mlp(stash, wgateup, wdown, dgateup, act_low, grads, total)
    spread(total, rows, parts, 1)


def second_stage(
    own_b, other, near_0, near_1, far, s_0, s_1, s_2, gains, stash_q, probs, wgateup, wdown, wout, wqkv,
    gateup, dqkv, dmid, p_0, p_1, p_2, p_3, p_4, p_5, p_6, p_7, full, dmixed, total,
):
    parts = (p_0, p_1, p_2, p_3, p_4, p_5, p_6, p_7)
    rows, blocks, gain = block_rows(), (own_b, other, near_0, near_1, far, s_0, s_1, s_2), gains[1:2, :]
    fill(full, rows, blocks, 0, lambda part: row_norm(part, gain).astype(BF))
    forward_mlp(wgateup, wdown, gateup, full, total)
    spread(total, rows, parts, 0)
    fill(dmid, rows, blocks, 1)
    backward_attention(stash_q, probs, wqkv, wout, dqkv, dmid, dmixed, total)
    spread(total, rows, parts, 1)


def backward_probs(flags, held, fetched, qkv, mixed, probs):
    pick_stash(moved_stash(flags), fetched, (None, held), (None, qkv))
    for h in range(2):
        rows = pl.ds(h * HEAD, HEAD)
        probs[h] = probs_of(qkv[1, rows, :], qkv[0, rows, :])
        mixed[rows, :] = dot(qkv[2, rows, :], probs[h].astype(BF), NN).astype(BF)


def mlp_weights(own_b, other, near_0, near_1, far, s_0, s_1, s_2, gains, dgateup, act_low, grads, grad_gateup, grad_down, full):
    gain = gains[1:2, :]
    grad_down[...] = dot(act_low[...], grads[...], TN).astype(BF)
    fill(full, block_rows(), (own_b, other, near_0, near_1, far, s_0, s_1, s_2), 3, lambda part: row_norm(part, gain).astype(BF))
    for c in range(2):
        grad_gateup[c] = dot(full[...], dgateup[c], TN).astype(BF)


def attention_weights(
    own_b, other, near_0, near_1, far, s_0, s_1, s_2, gains, dqkv, mixed, dmid, wqkv, grad_qkv, grad_out, gain_terms, full,
):
    gain = gains[0:1, :]
    grad_out[...] = dot(mixed[...], dmid[...], NN).astype(BF)
    fill(full, block_rows(), (own_b, other, near_0, near_1, far, s_0, s_1, s_2), 2, lambda part: row_norm(part, gain).astype(BF))
    terms = jnp.zeros((1, D), F32)
    for c in range(3):
        grad = dot(dqkv[c], full[...], NN)
        grad_qkv[c] = grad.astype(BF)
        terms += jnp.sum(grad * wqkv[c].astype(F32), axis=0, keepdims=True)
    gain_terms[...] = terms / gain


def total_of(own, near, second, which):
    return own[which].astype(F32) + near[which].astype(F32) + second[which].astype(F32)


def norm_back(source, gain, upstream):
    values = source.astype(F32)
    inverse = unit_scale(values)
    normal = values * inverse
    scaled = upstream * gain
    inner = jnp.mean(scaled * normal, axis=-1, keepdims=True)
    return inverse * (scaled - normal * inner), upstream * normal


def middle(flags, held, fetched, x, dy, own, near, second, gains, out, terms, stash):
    pick_stash(moved_stash(flags), fetched, (held, None), (stash, None))
    out[0] = (x[...].astype(F32) + total_of(own, near, second, 0)).astype(BF)
    back, products = norm_back(stash[1], gains[1:2, :], total_of(own, near, second, 1))
    out[1] = (dy[...].astype(F32) + back).astype(BF)
    out[2] = stash[0]
    out[3] = stash[1]
    terms[...] = jnp.sum(products, axis=0, keepdims=True)


def last(mids, own, near, second, gains, layer_out, dinput):
    layer_out[...] = (mids[0].astype(F32) + total_of(own, near, second, 0)).astype(BF)
    back, _ = norm_back(mids[2], gains[0:1, :], total_of(own, near, second, 1))
    dinput[...] = (mids[1].astype(F32) + back).astype(BF)


def shifted(value, by):
    count = lax.axis_size("section")
    pairs = [(i, i + by) for i in range(count) if 0 <= i + by < count]
    return lax.ppermute(value, "section", pairs)


def mirrored(value):
    count = lax.axis_size("section")
    return lax.ppermute(value, "section", [(i, count - 1 - i) for i in range(count)])


def on_device(
    layer_inputs, output_grads, held_inputs, held_qkv, held_gateup, swapped_pairs,
    w_qkv, w_out, w_gateup, w_down, norm_gains,
):
    layer_in, dy = layer_inputs[0], output_grads[0]
    wqkv = jnp.swapaxes(w_qkv[0], 1, 2)
    held_q = jnp.swapaxes(held_qkv[0], 1, 2)
    wout, wgateup, wdown, gains = w_out[0], w_gateup[0], w_down[0], norm_gains[0]
    held_x, held_g = held_inputs[0], held_gateup[0]
    mega = 256 * 1536 * 2
    full, total = pltpu.VMEM((256, D), BF), pltpu.VMEM((256, D), F32)
    per_head, pair = pltpu.VMEM((192, 256), BF), pltpu.VMEM((2, 32, D), BF)

    own = call(
        stack, "stack", [shape(2, 32, D)], [pltpu.SemaphoreType.DMA(())] * 2, 8192, (layer_in, dy), (0, 1)
    )[0]
    fetched_g = mirrored(after(held_g, own))
    weights = [after(wqkv, own), wout, held_g, wdown, wgateup]
    wqkv, wout, held_g, wdown, wgateup = call(
        bring, "bring", [pltpu.VMEM(w.shape, w.dtype) for w in weights],
        [pltpu.SemaphoreType.DMA(()) for _ in weights], 8192, weights, (0, 1, 2, 3, 4),
    )
    (packed,) = call(pack_held, "pack_held", [shape(STASH, 128)], [], 8192, (held_x, after(held_q, own)))
    blocks = gather(own, (wqkv, packed), lambda _: (fetched_g,))
    fetched = mirrored(after(packed, blocks[3]))

    qkv, dgateup, act_low, grads, *parts = call(
        first_stage, "first_stage",
        [shape(3, 192, 256), shape(2, 256, 384), shape(256, 384), shape(256, D)] + SPREAD,
        [full, per_head, total, pltpu.VMEM((2, 256, 384), BF)],
        mega * 2050,
        (swapped_pairs, *blocks, gains, fetched_g, wqkv, wout, held_g, wdown, wgateup),
    )
    parts[7] = after(parts[7], fetched)
    _, _, far, other = start_sums(parts)
    sums = end_sums(parts, last_held(parts, far), other)
    mids, mid_terms = call(
        middle, "middle", [shape(4, 32, D), shape(1, D, dtype=F32)], [pair],
        32 * D * 40, (swapped_pairs, held_x, fetched, layer_in, dy, *sums, gains),
    )

    stash_q, mixed, probs = call(
        backward_probs, "backward_probs",
        [shape(3, 192, 256), shape(192, 256), shape(2, 256, 256, dtype=F32)], [],
        1024, (swapped_pairs, held_q, fetched),
    )
    blocks = gather(mids, (probs,))
    (packed,) = call(pack_new, "pack_new", [shape(STASH, 128)], [pair], 1024, (layer_in, mids, qkv))
    moved = mirrored(after(packed, blocks[2]))

    gateup, dqkv, dmid, *parts = call(
        second_stage, "second_stage",
        [shape(2, 256, 384), shape(3, 192, 256), shape(256, D)] + SPREAD,
        [full, per_head, total],
        1024,
        (*blocks, gains, stash_q, probs, wgateup, wdown, wout, wqkv),
    )

    grad_qkv, grad_out, in_terms = call(
        attention_weights, "attention_weights",
        [shape(3, 192, D), shape(192, D), shape(1, D, dtype=F32)], [full],
        1024, (*blocks, gains, dqkv, mixed, dmid, wqkv),
    )
    grad_gateup, grad_down = call(
        mlp_weights, "mlp_weights",
        [shape(2, D, 384), shape(384, D)], [full],
        1024, (*blocks, gains, dgateup, act_low, after(grads, gateup)),
    )
    parts[7] = after(parts[7], moved, in_terms, grad_down)
    held_2, held_1, far, other = start_sums(parts)
    moved_gateup = mirrored(after(gateup, other))
    terms = add_across(jnp.concatenate([in_terms, mid_terms]), 1)
    terms = add_across(after(terms, held_2), 2)
    stash_inputs, stash_qkv = call(
        stash_out, "stash_out", [shape(*part) for part in PARTS], [pair],
        1024, (swapped_pairs, after(moved, held_2), layer_in, mids, qkv),
    )
    held_0 = after(last_held(parts, far), terms, stash_inputs)
    grad_gains = add_across(after(terms, held_0), 4)
    sums = end_sums(parts, held_0, other)
    layer_out, dinput = call(
        last, "last", [shape(32, D), shape(32, D)], [],
        32 * D * 40, (mids, *sums, gains),
    )
    forward_sent = shifted(layer_out, 1)
    backward_sent = shifted(dinput, -1)
    (stash_gateup,) = call(
        stash_out_last, "stash_out_last", [shape(2, 256, 384)], [],
        1024, (swapped_pairs, moved_gateup, gateup),
    )

    return (
        forward_sent[None],
        backward_sent[None],
        stash_inputs[None],
        jnp.swapaxes(stash_qkv, 1, 2)[None],
        stash_gateup[None],
        jnp.swapaxes(grad_qkv, 1, 2)[None],
        grad_out[None],
        grad_gateup[None],
        grad_down[None],
        grad_gains[None],
    )


def solution(mesh):
    in_specs = (
        P("section", "tensor", None),
        P("section", "tensor", None),
        P("section", None, "tensor", None),
        P("section", None, None, "tensor"),
        P("section", None, None, "tensor"),
        P(),
        P("section", None, None, "tensor"),
        P("section", "tensor", None),
        P("section", None, None, "tensor"),
        P("section", "tensor", None),
        P("section", None, None),
    )
    out_specs = (
        P("section", "tensor", None),
        P("section", "tensor", None),
        P("section", None, "tensor", None),
        P("section", None, None, "tensor"),
        P("section", None, None, "tensor"),
        P("section", None, None, "tensor"),
        P("section", "tensor", None),
        P("section", None, None, "tensor"),
        P("section", "tensor", None),
        P("section", None, None),
    )
    return jax.shard_map(
        on_device, mesh=mesh, in_specs=in_specs, out_specs=out_specs, check_vma=False
    )
```
